512 devices in a mesh: kv: 8 (over z), wide: 64 (over x, y, core).
Axes of the slice: x: 4, y: 8, z: 8, core: 2. Of those that a mesh axis runs over, the one named last changes fastest.
Arguments:
- hidden_input: bfloat16 [192, 16384], P(None, 'kv'), may hold values from -6 to 6
- input_norm_gain: float32 [16384], P('kv'), may hold values from 0.25 to 1.75
- joint_projection_weight: bfloat16 [16384, 18432], P('kv', 'wide'), may hold values from -0.046875 to 0.046875
- output_weight: bfloat16 [16384, 16384], P('kv', 'wide'), may hold values from -0.046875 to 0.046875
- key_cache: bfloat16 [192, 8, 512, 128], P('wide', 'kv'), may hold values from -210 to 210
- value_cache: bfloat16 [192, 8, 512, 128], P('wide', 'kv'), may hold values from -6 to 6
- joint_down_weight: bfloat16 [64, 16384, 24], P('wide', 'kv'), may hold values from -0.046875 to 0.046875
- query_up_weight: bfloat16 [64, 8, 16384], P('wide', None, 'kv'), may hold values from -2 to 2
- key_value_up_weight: bfloat16 [64, 2, 8, 1024], P('wide', None, None, 'kv'), may hold values from -2 to 2
- output_down_weight: bfloat16 [64, 16384, 8], P('wide', 'kv'), may hold values from -0.046875 to 0.046875
- output_up_weight: bfloat16 [64, 8, 16384], P('wide'), may hold values from -2 to 2
- row_adapter_index: int32 [192], replicated, may hold values from 0 to 63
- adapter_owner_slot: int32 [64], replicated, may hold values from 0 to 63, each once
- lengths: int32 [192], P('wide'), may hold values from 64 to 512, as said below
Outputs:
- out: bfloat16 [192, 16384], P('kv', 'wide')
The draws below stay inside these ranges and needn't reach their ends.
Inputs may be any that keep to these rules, and one draw needn't show every extreme that they name: Row lengths; at least one row has exactly 512. `adapter_owner_slot`: each adapter's owner slot, a permutation.
All inputs are finite; a program needn't handle non-finite values.
Results may differ from the reference program's by a relative error of at most 0.019.
The reference program's roundings to bfloat16 on the way count: a program that leaves them out, or rounds other values in their place, can miss the bound.
Values may be sent and summed in bfloat16 or wider, within the bound.
A program may use at most 128 MiB of HBM per device.

```python
import math
import jax
import jax.numpy as jnp
import numpy as np
from jax import lax

MODEL_WIDTH = 16384
QUERY_HEADS = 128
KEY_HEADS = 8
HEAD_SIZE = 128
ADAPTER_RANK = 8
CACHE = 512
GROUP = 16
QKV = 18432
ADAPTER_TOTAL = 64
BATCH = 192


def draw_lengths(key, part):
    lens = jax.random.randint(key, (BATCH,), CACHE // 8, CACHE + 1)
    full_row = jax.random.randint(jax.random.fold_in(key, 7), (), 0, BATCH)
    return jnp.where(jnp.arange(BATCH) == full_row, CACHE, lens).astype(jnp.int32)


def draw_key_cache(key, part):
    array_shape = (BATCH, KEY_HEADS, CACHE, HEAD_SIZE)
    base_output = jax.random.normal(key, array_shape, jnp.float32)
    return base_output.astype(jnp.bfloat16)


def set_ends(values, key, least, high):
    spot = [jax.random.randint(jax.random.fold_in(key, axis), (), 0, length) for axis, length in enumerate(values.shape)]
    main_axis = values.shape.index(max(values.shape))
    beside = spot[:main_axis] + [(spot[main_axis] + 1) % values.shape[main_axis]] + spot[main_axis + 1:]
    return values.at[tuple(spot)].set(least).at[tuple(beside)].set(high)


def level_of(stream_key, extent, shards, least, high):
    gain, own = 1.0, jax.random.fold_in(stream_key, 6)
    for axis_at, blocks in shards:
        heights = jnp.exp(jax.random.uniform(jax.random.fold_in(own, axis_at), (blocks,), jnp.float32, least / len(shards), high / len(shards)))
        gain = gain * jnp.repeat(heights, extent[axis_at] // blocks).reshape([-1 if axis == axis_at else 1 for axis in range(len(extent))])
    return gain


def rank_bounds(number_of, slope):
    portions = [(1 << 20) // math.isqrt(standing ** slope) + 1 for standing in range(1, number_of + 1)]
    scale = 1 + sum(portions) // (1 << 30)
    return np.cumsum(np.array([max(1, weight // scale) for weight in portions]))


def ranked(own_key, dims, count, lean):
    grid = rank_bounds(count, lean)
    lot = jax.random.randint(jax.random.fold_in(own_key, 1), dims, 0, int(grid[count - 1]))
    rank = jnp.searchsorted(jnp.asarray(grid, jnp.int32), lot, side="right")
    return jax.random.permutation(jax.random.fold_in(own_key, 2), count)[rank].astype(jnp.int32)


def normal_values(stream_key, shape, scale, most, pieces=(), kind=jnp.bfloat16):
    entries = jax.random.normal(stream_key, shape, jnp.float32) * scale
    if len(pieces) > 0:
        entries = level_of(stream_key, shape, pieces, -0.22, 0.18) * entries
    return jnp.clip(entries, min=-most, max=most).astype(kind)


def setup_inputs(seed: int = 0) -> dict:
    key_of = jax.random.split(jax.random.key(seed), 15)
    hidden_input = normal_values(key_of[0], (BATCH, MODEL_WIDTH), 1.0, 6.0, ((1, 8),))
    input_norm_gain = jnp.clip(1.0 + 0.15 * jax.random.normal(key_of[1], (MODEL_WIDTH,), jnp.float32), 0.25, 1.75)
    joint_projection_weight = normal_values(key_of[2], (MODEL_WIDTH, QKV), MODEL_WIDTH ** -0.5, 0.046875, ((0, 8), (1, 64)))
    output_weight = normal_values(key_of[3], (QUERY_HEADS * HEAD_SIZE, MODEL_WIDTH), (QUERY_HEADS * HEAD_SIZE) ** -0.5, 0.046875, ((0, 8), (1, 64)))
    key_cache = draw_key_cache(jax.random.fold_in(key_of[14], 71), 0)
    value_cache = normal_values(key_of[5], (BATCH, KEY_HEADS, CACHE, HEAD_SIZE), 1.0, 6.0, ((0, 64), (1, 8)))
    joint_down_weight = normal_values(key_of[6], (ADAPTER_TOTAL, MODEL_WIDTH, 3 * ADAPTER_RANK), MODEL_WIDTH ** -0.5, 0.046875, ((0, 64), (1, 8)))
    query_up_weight = normal_values(key_of[7], (ADAPTER_TOTAL, ADAPTER_RANK, QUERY_HEADS * HEAD_SIZE), ADAPTER_RANK ** -0.5, 2.0, ((0, 64), (2, 8)))
    key_value_up_weight = normal_values(key_of[8], (ADAPTER_TOTAL, 2, ADAPTER_RANK, KEY_HEADS * HEAD_SIZE), ADAPTER_RANK ** -0.5, 2.0, ((0, 64), (3, 8)))
    output_down_weight = normal_values(key_of[9], (ADAPTER_TOTAL, QUERY_HEADS * HEAD_SIZE, ADAPTER_RANK), (QUERY_HEADS * HEAD_SIZE) ** -0.5, 0.046875, ((0, 64), (1, 8)))
    output_up_weight = normal_values(key_of[10], (ADAPTER_TOTAL, ADAPTER_RANK, MODEL_WIDTH), ADAPTER_RANK ** -0.5, 2.0, ((0, 64),))
    row_adapter_index = set_ends(ranked(key_of[11], (BATCH,), ADAPTER_TOTAL, 2), jax.random.fold_in(key_of[11], 3), 0, ADAPTER_TOTAL - 1).astype(jnp.int32)
    adapter_owner_slot = jax.random.permutation(key_of[12], ADAPTER_TOTAL).astype(jnp.int32)
    lengths = draw_lengths(jax.random.fold_in(key_of[14], 71), 0)
    return {"hidden_input": hidden_input, "input_norm_gain": input_norm_gain, "joint_projection_weight": joint_projection_weight, "output_weight": output_weight, "key_cache": key_cache, "value_cache": value_cache, "joint_down_weight": joint_down_weight, "query_up_weight": query_up_weight, "key_value_up_weight": key_value_up_weight, "output_down_weight": output_down_weight, "output_up_weight": output_up_weight, "row_adapter_index": row_adapter_index, "adapter_owner_slot": adapter_owner_slot, "lengths": lengths}


rope_base = 500000.0
adapter_scale = 2.0

def rotate(values, positions):
    half = values.shape[-1] // 2
    freq = rope_base ** (-jnp.arange(half, dtype=jnp.float32) * 2.0 / values.shape[-1])
    angle = positions.astype(jnp.float32)[:, None] * freq[None, :]
    array_shape = (angle.shape[0],) + (1,) * (values.ndim - 2) + (half,)
    cosine = jnp.cos(angle).reshape(array_shape)
    sine = jnp.sin(angle).reshape(array_shape)
    first = values[..., :half]
    second = values[..., half:]
    return jnp.concatenate([first * cosine - second * sine, second * cosine + first * sine], axis=-1)

def reference(hidden_input, input_norm_gain, joint_projection_weight, output_weight, key_cache, value_cache, joint_down_weight, query_up_weight, key_value_up_weight, output_down_weight, output_up_weight, row_adapter_index, adapter_owner_slot, lengths):
    widened = hidden_input.astype(jnp.float32)
    scale = lax.rsqrt(lax.optimization_barrier(jnp.sum(widened * widened, axis=1)) / MODEL_WIDTH + 1e-05)
    scaled_hidden = (widened * input_norm_gain.astype(jnp.float32)[None, :]).astype(jnp.bfloat16)
    owner_slots = adapter_owner_slot[row_adapter_index].astype(jnp.int32)
    base_output = jnp.dot(scaled_hidden, joint_projection_weight, preferred_element_type=jnp.float32) * scale[:, None]
    reduced_everywhere = jnp.einsum('qy,tya->qta', scaled_hidden.astype(jnp.float32), joint_down_weight.astype(jnp.float32))
    reduced_hidden = jnp.take_along_axis(reduced_everywhere, owner_slots[:, None, None], axis=1)[:, 0]
    reduced_hidden = (reduced_hidden * scale[:, None]).astype(jnp.bfloat16).astype(jnp.float32)
    query_change = jnp.einsum('xq,xqi->xi', reduced_hidden[:, :ADAPTER_RANK], query_up_weight[owner_slots].astype(jnp.float32))
    key_change = jnp.einsum('xq,xqi->xi', reduced_hidden[:, ADAPTER_RANK:2 * ADAPTER_RANK], key_value_up_weight[owner_slots, 0].astype(jnp.float32))
    value_change = jnp.einsum('xq,xqi->xi', reduced_hidden[:, 2 * ADAPTER_RANK:], key_value_up_weight[owner_slots, 1].astype(jnp.float32))
    batch_rows = hidden_input.shape[0]
    adapter_change = jnp.concatenate([query_change.reshape(batch_rows, KEY_HEADS, -1), key_change.reshape(batch_rows, KEY_HEADS, -1), value_change.reshape(batch_rows, KEY_HEADS, -1)], axis=2)
    merged_output = base_output.reshape(batch_rows, KEY_HEADS, -1) + adapter_scale * adapter_change
    width = GROUP * HEAD_SIZE
    query_vector = rotate(merged_output[:, :, :width].reshape(batch_rows, KEY_HEADS, GROUP, HEAD_SIZE), lengths).astype(jnp.bfloat16).astype(jnp.float32)
    fresh_key = rotate(merged_output[:, :, width:width + HEAD_SIZE], lengths).astype(jnp.bfloat16).astype(jnp.float32)
    value_new = merged_output[:, :, width + HEAD_SIZE:].astype(jnp.bfloat16).astype(jnp.float32)
    inverse_root = jnp.sqrt(jnp.float32(HEAD_SIZE))
    scores = jnp.einsum('bkgd,bkld->bkgl', query_vector, key_cache.astype(jnp.float32)) / inverse_root
    valid = jnp.arange(CACHE, dtype=jnp.int32)[None, :] < lengths[:, None]
    scores = jnp.where(valid[:, None, None, :], scores, -jnp.inf)
    fresh_score = jnp.einsum('ajtm,ajm->ajt', query_vector, fresh_key) / inverse_root
    top = jnp.maximum(lax.optimization_barrier(jnp.max(scores, axis=-1)), fresh_score)
    expd = jnp.exp(scores - top[..., None])
    exp_new = jnp.exp(fresh_score - top)
    total = lax.optimization_barrier(jnp.sum(expd, axis=-1)) + exp_new
    probs = (expd / total[..., None]).astype(jnp.bfloat16).astype(jnp.float32)
    prob_new = (exp_new / total).astype(jnp.bfloat16).astype(jnp.float32)
    attention_output = jnp.einsum('bkgl,bkld->bkgd', probs, value_cache.astype(jnp.float32)) + prob_new[..., None] * value_new[:, :, None, :]
    attention_output = attention_output.astype(jnp.bfloat16).reshape(batch_rows, QUERY_HEADS * HEAD_SIZE)
    output_baseline = jnp.dot(attention_output, output_weight, preferred_element_type=jnp.float32)
    output_everywhere = jnp.einsum('iv,gvl->igl', attention_output.astype(jnp.float32), output_down_weight.astype(jnp.float32))
    output_reduced = jnp.take_along_axis(output_everywhere, owner_slots[:, None, None], axis=1)[:, 0].astype(jnp.bfloat16).astype(jnp.float32)
    output_change = jnp.einsum('pc,pcw->pw', output_reduced, output_up_weight[owner_slots].astype(jnp.float32))
    return (output_baseline + adapter_scale * output_change).astype(jnp.bfloat16)
```

```python
import math

import jax
import jax.numpy as jnp
import numpy as np
from jax import lax
from jax.experimental import pallas as pl
from jax.experimental.pallas import tpu as pltpu
from jax.sharding import PartitionSpec as P

MODEL_WIDTH = 16384
ROPE_BASE = 500000.0
MESH = pl.DeviceIdType.MESH
NT = (((1,), (1,)), ((), ()))
F32 = jnp.float32
BF16 = jnp.bfloat16


def tile_rank(part):
    for shift in (8, 16, 32, 64):
        part = part + pltpu.roll(part, shift, 1)
    return part


def one_hot_rows(rows, first_lane, slots):
    lane = lax.broadcasted_iota(jnp.int32, (24, 128), 1)
    if first_lane:
        rows = pltpu.roll(rows, 128 - first_lane, 1)
    tiled = tile_rank(jnp.where(lane < 8, rows, 0.0))
    group = lax.shift_right_logical(lane, 3)
    return jnp.concatenate(
        [jnp.where(slots == group + 16 * m, tiled, 0.0) for m in range(4)], axis=1
    ).astype(BF16)


def pack_rows(rows):
    return (
        rows[0:8] + pltpu.roll(rows[8:16], 32, 1) + pltpu.roll(rows[16:24], 64, 1)
    )


def unpack_rows(packed):
    return jnp.concatenate(
        [packed, pltpu.roll(packed, 96, 1), pltpu.roll(packed, 64, 1)], axis=0
    )


def layer(
    hidden, gain, weight_t, out_weight, key_cache, value_cache, down_t, query_up,
    key_value_up, out_down_t, out_up, freq, row_adapter, owner_slot, lengths,
    out,
    hid, gain_v, gained, wt, down3, part, tiny, recv1, recv2, ups, oups, u_all, uo_all,
    y_stage, recv_y, x_stage, recv_x, stage5, recv5, heads, keys, values, freq_v,
    att_f, att_b, recv_a, pack_f, lhs, wo, odown3, po, otiny, recv_o1, recv_o2,
    oy_stage, recv_oy, ox_stage, recv_ox,
    load_sem, s1, r1, s2, r2, su, ru, suo, ruo, szu, rzu, szo, rzo, sy, ry, sx, rx,
    s5, r5, sa, ra, sg, rg, sf, rf, so1, ro1, so2, ro2, soy, roy, sox, rox,
    self_sem,
):
    k = lax.axis_index("kv")
    w = lax.axis_index("wide")
    w_hi = lax.div(w, 8)
    w_lo = lax.rem(w, 8)
    x = lax.div(w, 16)
    c = lax.rem(w, 2)
    y = lax.rem(lax.div(w, 2), 8)
    g = 2 * x + c
    chunk_shift = 32 * lax.rem(w_lo, 4)

    wt[0:96, :] = jnp.zeros((96, 2048), BF16)
    wt[288:384, :] = jnp.zeros((96, 2048), BF16)
    down3[...] = jnp.zeros((128, 2048), BF16)
    odown3[...] = jnp.zeros((128, 2048), BF16)

    def load(src, dst, index):
        copy = pltpu.make_async_copy(src, dst, load_sem.at[index])
        copy.start()
        return copy

    load_hidden = [load(hidden, hid, 0), load(gain, gain_v, 1)]
    load_down = [load(down_t.at[0], down3.at[pl.ds(32 * i, 24)], 2 + i) for i in range(3)]
    load_weight = load(weight_t, wt.at[pl.ds(pl.multiple_of(chunk_shift, 32), 288)], 5)
    load_ups = [
        load(query_up.at[0], ups.at[:, pl.ds(0, 2048)], 6),
        load(key_value_up.at[0, 0], ups.at[:, pl.ds(2048, 128)], 7),
        load(key_value_up.at[0, 1], ups.at[:, pl.ds(2176, 128)], 8),
        load(out_up.at[0, :, pl.ds(pl.multiple_of(2048 * k, 2048), 2048)], oups, 9),
    ]
    load_cache = [load(key_cache.at[:, 0], keys, 10), load(value_cache.at[:, 0], values, 11)]
    load_out = [load(out_weight, wo, 12)] + [
        load(out_down_t.at[0], odown3.at[pl.ds(32 * i, 8)], 13 + i) for i in range(3)
    ]
    load_freq = load(freq, freq_v, 16)

    def z_peer(d):
        return (lax.rem(k + d, 8), w)

    def y_peer(d):
        return (k, 16 * x + 2 * lax.rem(y + d, 8) + c)

    def g_peer(d):
        other = lax.rem(g + d, 8)
        return (k, 16 * lax.div(other, 2) + 2 * y + lax.rem(other, 2))

    def t_peer(i):
        return (w_hi, 8 * k + i)

    def before(pos, d, n=8):
        return lax.rem(pos + n - d, n)

    in_set = w_hi == k

    def t_other(i):
        return jnp.logical_or(jnp.logical_not(in_set), w_lo != i)

    barrier = pltpu.get_barrier_semaphore()
    for d in range(1, 8):
        for peer in (z_peer(d), y_peer(d), g_peer(d)):
            pl.semaphore_signal(barrier, inc=1, device_id=peer, device_id_type=MESH)
    for i in range(8):
        @pl.when(t_other(i))
        def _(i=i):
            pl.semaphore_signal(barrier, inc=1, device_id=t_peer(i), device_id_type=MESH)

    def remote(src, dst, send, recv, peer):
        return pltpu.make_async_remote_copy(
            src_ref=src, dst_ref=dst, send_sem=send, recv_sem=recv,
            device_id=peer, device_id_type=MESH,
        )

    sent = []

    def send_line(src_of, dst, send, recv, peer_of, pos):
        for d in range(1, 8):
            copy = remote(src_of(d), dst.at[pos], send.at[d], recv.at[d], peer_of(d))
            copy.start()
            sent.append(copy)

    def wait_line(dst, send, recv, peer_of, pos):
        for d in range(1, 8):
            slot = dst.at[before(pos, d)]
            remote(slot, slot, send.at[d], recv.at[d], peer_of(d)).wait_recv()

    def t_copies(src_of, dst, send, recv):
        copies = []
        for i in range(8):
            copies.append(remote(src_of(i), dst, send.at[i], recv.at[w_lo], t_peer(i)))
        return copies

    def t_start(src_of, dst, send, recv, own):
        for i, copy in enumerate(t_copies(src_of, dst, send, recv)):
            @pl.when(t_other(i))
            def _(copy=copy):
                copy.start()

            @pl.when(jnp.logical_not(t_other(i)))
            def _(i=i):
                local = pltpu.make_async_copy(src_of(i), dst, own)
                local.start()
                local.wait()

    def t_wait_recv(slot_of, send, recv):
        for j in range(8):
            slot = slot_of(j)

            @pl.when(t_other(j))
            def _(j=j, slot=slot):
                remote(slot, slot, send.at[j], recv.at[j], t_peer(j)).wait_recv()

    def t_wait_send(src_of, dst, send, recv):
        for i, copy in enumerate(t_copies(src_of, dst, send, recv)):
            @pl.when(t_other(i))
            def _(copy=copy):
                copy.wait_send()

    for copy in load_hidden:
        copy.wait()
    wide_h = hid[...].astype(F32)
    gained[...] = (wide_h * gain_v[...]).astype(BF16)
    squares = jnp.sum(wide_h * wide_h, axis=1, keepdims=True)
    for copy in load_down:
        copy.wait()
    reduced = lax.dot_general(gained[...], down3[...], NT, preferred_element_type=F32)
    lane192 = lax.broadcasted_iota(jnp.int32, (192, 128), 1)
    reduced = jnp.where(lax.rem(lane192, 32) == 24, squares, reduced)
    lane8 = lax.broadcasted_iota(jnp.int32, (8, 128), 1)
    for b in range(8):
        r = 24 * b
        tiny[b] = jnp.where(
            lane8 < 32, reduced[r : r + 8],
            jnp.where(lane8 < 64, reduced[r + 8 : r + 16],
                      jnp.where(lane8 < 96, reduced[r + 16 : r + 24], 0.0)),
        )
    recv1[k] = tiny[k]

    pl.semaphore_wait(barrier, jnp.where(in_set, 28, 29))
    send_line(lambda d: tiny.at[lax.rem(k + d, 8)], recv1, s1, r1, z_peer, k)

    for copy in load_ups:
        copy.wait()

    def up_chunk(i):
        return ups.at[:, pl.ds(128 * (2 * i + i // 4), 384)]

    def oup_chunk(i):
        return oups.at[:, pl.ds(256 * i, 256)]

    t_start(up_chunk, u_all.at[w], su, ru, self_sem.at[0])

    load_weight.wait()
    part[...] = lax.dot_general(
        gained[...], wt[...], NT, preferred_element_type=F32
    ).reshape(8, 24, 384)
    send_line(lambda d: part.at[lax.rem(k + d, 8)], recv2, s2, r2, z_peer, k)
    recv2[k] = part[k]

    t_start(oup_chunk, uo_all.at[w], suo, ruo, self_sem.at[1])
    t_wait_recv(lambda j: u_all.at[8 * k + j], su, ru)
    own_u = u_all.at[pl.ds(8 * k, 8)]
    for d in range(1, 8):
        copy = remote(own_u, own_u, szu.at[d], rzu.at[d], z_peer(d))
        copy.start()
        sent.append(copy)

    row24 = lax.broadcasted_iota(jnp.int32, (24, 128), 0)
    slots = jnp.zeros((24, 128), jnp.int32)
    slots_o = jnp.zeros((24, 128), jnp.int32)
    for b in range(24):
        slot = owner_slot[row_adapter[24 * k + b]]
        yy, cc, rr = b // 6, (b // 3) % 2, b % 3
        slots = jnp.where(row24 == b, slot, slots)
        slots_o = jnp.where(row24 == 12 * cc + 3 * yy + rr, slot, slots_o)
    lane24 = lax.broadcasted_iota(jnp.int32, (24, 128), 1)

    wait_line(recv1, s1, r1, z_peer, k)
    rows = unpack_rows(jnp.sum(recv1[...], axis=0))
    scale = lax.rsqrt(rows[:, 24:25] / MODEL_WIDTH + 1e-05)
    rows = (rows * scale).astype(BF16).astype(F32)
    rows = jnp.where(jnp.logical_and(slots == w, lane24 < 24), rows, 0.0)
    y_stage[...] = pack_rows(rows)
    send_line(lambda d: y_stage, recv_y, sy, ry, y_peer, y)
    recv_y[y] = y_stage[...]
    wait_line(recv_y, sy, ry, y_peer, y)
    x_stage[...] = jnp.sum(recv_y[...], axis=0)
    send_line(lambda d: x_stage, recv_x, sx, rx, g_peer, g)
    recv_x[g] = x_stage[...]
    wait_line(recv_x, sx, rx, g_peer, g)
    shrink = unpack_rows(jnp.sum(recv_x[...], axis=0))
    left_q = one_hot_rows(shrink, 0, slots)
    left_k = one_hot_rows(shrink, 8, slots)
    left_v = one_hot_rows(shrink, 16, slots)

    for d in range(1, 8):
        slot = u_all.at[pl.ds(8 * before(k, d), 8)]
        remote(slot, slot, szu.at[d], rzu.at[d], z_peer(d)).wait_recv()
    u_mat = u_all[...].reshape(512, 384)
    delta = jnp.dot(left_q, u_mat, preferred_element_type=F32)
    delta_k = jnp.dot(left_k, u_mat[:, 128:256], preferred_element_type=F32)
    delta_v = jnp.dot(left_v, u_mat[:, 256:384], preferred_element_type=F32)
    last = w_lo == 7
    delta = jnp.concatenate(
        [
            delta[:, 0:128],
            jnp.where(last, delta_k, delta[:, 128:256]),
            jnp.where(last, delta_v, delta[:, 256:384]),
        ],
        axis=1,
    )
    lane384 = lax.broadcasted_iota(jnp.int32, (24, 384), 1)
    inside = jnp.logical_and(lane384 >= chunk_shift, lane384 < chunk_shift + 288)
    wait_line(recv2, s2, r2, z_peer, k)
    base = jnp.sum(recv2[...], axis=0) * scale
    merged = base + 2.0 * jnp.where(inside, delta, 0.0)
    for i in range(8):
        for t in range(3):
            stage5[i, :, t, :] = merged[3 * i : 3 * i + 3, 128 * t : 128 * t + 128]
    t_start(lambda i: stage5.at[i], recv5.at[w_lo], s5, r5, self_sem.at[2])

    t_wait_recv(lambda j: uo_all.at[8 * k + j], suo, ruo)
    own_uo = uo_all.at[pl.ds(8 * k, 8)]
    for d in range(1, 8):
        copy = remote(own_uo, own_uo, szo.at[d], rzo.at[d], z_peer(d))
        copy.start()
        sent.append(copy)

    load_freq.wait()
    for copy in load_cache:
        copy.wait()
    lane1 = lax.broadcasted_iota(jnp.int32, (1, 128), 1)
    turns = []
    for r in range(3):
        angle = lengths[r].astype(F32) * freq_v[...]
        sine = jnp.sin(angle)
        turns.append((jnp.cos(angle), jnp.where(lane1 < 64, -sine, sine)))
    t_wait_recv(lambda j: recv5.at[j], s5, r5)
    heads[...] = jnp.zeros((3, 24, 128), F32)
    for j in range(8):
        t = 2 * j + j // 4
        heads[:, t : t + 3, :] += recv5[j]
    root = 1.0 / math.sqrt(128.0)
    slot512 = lax.broadcasted_iota(jnp.int32, (16, 512), 1)
    for r in range(3):
        cosine, sine = turns[r]
        raw = heads[r]
        turned = (raw * cosine + pltpu.roll(raw, 64, 1) * sine).astype(BF16)
        query = turned[0:16]
        key_new = turned[16:17].astype(F32)
        value_new = raw[17:18].astype(BF16).astype(F32)
        scores = lax.dot_general(query, keys[r], NT, preferred_element_type=F32) * root
        scores = jnp.where(slot512 < lengths[r], scores, -jnp.inf)
        fresh = jnp.sum(query.astype(F32) * key_new, axis=1, keepdims=True) * root
        top = jnp.maximum(jnp.max(scores, axis=1, keepdims=True), fresh)
        expd = jnp.exp(scores - top)
        exp_new = jnp.exp(fresh - top)
        total = jnp.sum(expd, axis=1, keepdims=True) + exp_new
        probs = (expd / total).astype(BF16)
        prob_new = (exp_new / total).astype(BF16).astype(F32)
        attended = jnp.dot(probs, values[r], preferred_element_type=F32)
        attended = attended + prob_new * value_new
        for h in range(16):
            att_f[r : r + 1, 128 * h : 128 * h + 128] = attended[h : h + 1]
    att_f[3:4, :] = jnp.zeros((1, 2048), F32)
    att_b[...] = att_f[...].astype(BF16)

    send_line(lambda d: att_b, recv_a, sa, ra, y_peer, y)
    recv_a[y] = att_b[...]
    wait_line(recv_a, sa, ra, y_peer, y)
    for j in range(8):
        pack_f[3 * j : 3 * j + 3, :] = recv_a[j].astype(F32)[0:3]
    lhs[g] = pack_f[...].astype(BF16)
    sibling = (k, 16 * x + 2 * y + 1 - c)
    own = lhs.at[g]
    forward = []
    for d in range(1, 4):
        peer = (k, 16 * lax.rem(x + d, 4) + 2 * y + c)
        forward.append(remote(own, own, sg.at[d], rg.at[d], peer))
    forward.append(remote(own, own, sg.at[0], rg.at[0], sibling))
    for copy in forward:
        copy.start()
        sent.append(copy)
    for d in range(1, 4):
        far = before(x, d, 4)
        slot = lhs.at[2 * far + c]
        remote(slot, slot, sg.at[d], rg.at[d], sibling).wait_recv()
        copy = remote(slot, slot, sf.at[d], rf.at[d], sibling)
        copy.start()
        sent.append(copy)
    slot = lhs.at[2 * x + 1 - c]
    remote(slot, slot, sg.at[0], rg.at[0], sibling).wait_recv()
    for d in range(1, 4):
        slot = lhs.at[2 * before(x, d, 4) + 1 - c]
        remote(slot, slot, sf.at[d], rf.at[d], sibling).wait_recv()

    for copy in load_out:
        copy.wait()
    all_rows = lhs[...].reshape(192, 2048)
    oreduced = lax.dot_general(all_rows, odown3[...], NT, preferred_element_type=F32)

    def block_rows(array, b):
        r = 48 * (b // 2) + 12 * (b % 2)
        return jnp.concatenate([array[r : r + 12], array[r + 24 : r + 36]], axis=0)

    for b in range(8):
        mine = block_rows(oreduced, b)
        otiny[b] = jnp.where(
            lane8 < 32, mine[0:8],
            jnp.where(lane8 < 64, mine[8:16], jnp.where(lane8 < 96, mine[16:24], 0.0)),
        )
    send_line(lambda d: otiny.at[lax.rem(k + d, 8)], recv_o1, so1, ro1, z_peer, k)
    recv_o1[k] = otiny[k]
    product = jnp.dot(all_rows, wo[...], preferred_element_type=F32)
    for b in range(8):
        po[b] = block_rows(product, b).astype(BF16)
    send_line(lambda d: po.at[lax.rem(k + d, 8)], recv_o2, so2, ro2, z_peer, k)
    recv_o2[k] = po[k]

    wait_line(recv_o1, so1, ro1, z_peer, k)
    rows = unpack_rows(jnp.sum(recv_o1[...], axis=0)).astype(BF16).astype(F32)
    rows = jnp.where(jnp.logical_and(slots_o == w, lane24 < 8), rows, 0.0)
    oy_stage[...] = pack_rows(rows)
    send_line(lambda d: oy_stage, recv_oy, soy, roy, y_peer, y)
    recv_oy[y] = oy_stage[...]
    wait_line(recv_oy, soy, roy, y_peer, y)
    ox_stage[...] = jnp.sum(recv_oy[...], axis=0)
    send_line(lambda d: ox_stage, recv_ox, sox, rox, g_peer, g)
    recv_ox[g] = ox_stage[...]
    wait_line(recv_ox, sox, rox, g_peer, g)
    oshrink = unpack_rows(jnp.sum(recv_ox[...], axis=0))
    left_o = one_hot_rows(oshrink, 0, slots_o)
    for d in range(1, 8):
        slot = uo_all.at[pl.ds(8 * before(k, d), 8)]
        remote(slot, slot, szo.at[d], rzo.at[d], z_peer(d)).wait_recv()
    change = jnp.dot(left_o, uo_all[...].reshape(512, 256), preferred_element_type=F32)
    wait_line(recv_o2, so2, ro2, z_peer, k)
    total_out = jnp.sum(recv_o2[...].astype(F32), axis=0) + 2.0 * change
    to = lax.broadcasted_iota(jnp.int32, (24, 24), 0)
    frm = lax.broadcasted_iota(jnp.int32, (24, 24), 1)
    want = 12 * lax.rem(lax.div(to, 3), 2) + 3 * lax.div(to, 6) + lax.rem(to, 3)
    order = jnp.where(frm == want, 1.0, 0.0).astype(BF16)
    out[...] = jnp.dot(order, total_out.astype(BF16), preferred_element_type=F32).astype(BF16)

    for copy in sent:
        copy.wait_send()
    t_wait_send(up_chunk, u_all.at[w], su, ru)
    t_wait_send(oup_chunk, uo_all.at[w], suo, ruo)
    t_wait_send(lambda i: stage5.at[i], recv5.at[w_lo], s5, r5)


SCRATCH = [
    ((192, 2048), BF16), ((1, 2048), F32), ((192, 2048), BF16), ((384, 2048), BF16),
    ((128, 2048), BF16), ((8, 24, 384), F32), ((8, 8, 128), F32), ((8, 8, 128), F32),
    ((8, 24, 384), F32), ((8, 2304), BF16), ((8, 2048), BF16), ((64, 8, 384), BF16),
    ((64, 8, 256), BF16),
    ((8, 128), F32), ((8, 8, 128), F32), ((8, 128), F32), ((8, 8, 128), F32),
    ((8, 3, 3, 128), F32), ((8, 3, 3, 128), F32), ((3, 24, 128), F32),
    ((3, 512, 128), BF16), ((3, 512, 128), BF16), ((1, 128), F32),
    ((4, 2048), F32), ((4, 2048), BF16), ((8, 4, 2048), BF16), ((24, 2048), F32),
    ((8, 24, 2048), BF16), ((2048, 256), BF16), ((128, 2048), BF16),
    ((8, 24, 256), BF16), ((8, 8, 128), F32), ((8, 8, 128), F32), ((8, 24, 256), BF16),
    ((8, 128), F32), ((8, 8, 128), F32), ((8, 128), F32), ((8, 8, 128), F32),
]


def on_device(
    hidden_input, input_norm_gain, joint_projection_weight, output_weight, key_cache,
    value_cache, joint_down_weight, query_up_weight, key_value_up_weight,
    output_down_weight, output_up_weight, row_adapter_index, adapter_owner_slot, lengths,
):
    half = np.arange(64, dtype=np.float64)
    freq = np.float64(ROPE_BASE) ** (-half * 2.0 / 128.0)
    freq = jnp.asarray(np.concatenate([freq, freq])[None, :].astype(np.float32))
    any_spec = pl.BlockSpec(memory_space=pl.ANY)
    smem_spec = pl.BlockSpec(memory_space=pltpu.SMEM)
    sems = [pltpu.SemaphoreType.DMA((17,))] + [pltpu.SemaphoreType.DMA((8,))] * 33
    return pl.pallas_call(
        layer,
        out_shape=jax.ShapeDtypeStruct((24, 256), BF16),
        in_specs=[any_spec] * 12 + [smem_spec] * 3,
        out_specs=pl.BlockSpec(memory_space=pltpu.VMEM),
        scratch_shapes=[pltpu.VMEM(s, t) for s, t in SCRATCH] + sems,
        compiler_params=pltpu.CompilerParams(
            collective_id=0, has_side_effects=True, vmem_limit_bytes=40 * 1024 * 1024
        ),
        cost_estimate=pl.CostEstimate(
            flops=500_000_000, bytes_accessed=5_000_000, transcendentals=30_000
        ),
        name="layer",
    )(
        hidden_input, input_norm_gain[None, :], joint_projection_weight.T, output_weight,
        key_cache, value_cache, jnp.swapaxes(joint_down_weight, 1, 2), query_up_weight,
        key_value_up_weight, jnp.swapaxes(output_down_weight, 1, 2), output_up_weight,
        freq, row_adapter_index, adapter_owner_slot, lengths,
    )


def solution(mesh):
    in_specs = (
        P(None, "kv"), P("kv"), P("kv", "wide"), P("kv", "wide"),
        P("wide", "kv", None, None), P("wide", "kv", None, None), P("wide", "kv", None),
        P("wide", None, "kv"), P("wide", None, None, "kv"), P("wide", "kv", None),
        P("wide", None, None), P(), P(), P("wide"),
    )
    return jax.shard_map(
        on_device, mesh=mesh, in_specs=in_specs, out_specs=P("kv", "wide"), check_vma=False
    )
```
